32 devices in a mesh: group: 2 (over y), member: 16 (over z, x, core).
Axes of the slice: x: 2, y: 2, z: 4, core: 2. Of those that a mesh axis runs over, the one named last changes fastest.
Arguments:
- student: bfloat16 [12288, 768], P(('group', 'member')), may hold values from -0.29882812 to 0.29882812
- teacher: bfloat16 [12288, 1024], P(('group', 'member')), may hold values from -14 to 14
- counts: int32 [12288], P(('group', 'member')), may hold values from 1 to 7, as said below
- plan: int32 [2, 16, 5], P('group', 'member'), may hold values from 0 to 1, as said below
Outputs:
- grad_student: float32 [12288, 768], P(('group', 'member'))
- loss: float32 [], replicated
The draws below stay inside these ranges and needn't reach their ends.
Inputs may be any that keep to these rules, and one draw needn't show every extreme that they name: `counts`: each row's count is a whole number from 1 up. The pairing is symmetric: plan[g, m, 2 + k - 1] equals plan[g, (m + k) mod 16, k - 1] for k = 1 to 2, and plan[g, m, 4] equals plan[g xor 1, m, 4].
All inputs are finite; a program needn't handle non-finite values.
Results may differ from the reference program's by a relative error of at most 0.0046.
Values may be sent and summed in bfloat16 or wider, within the bound.
No kernel may reach another device: no remote copies, remote signals or barrier semaphores. Data moves between devices by JAX's collectives and lax.ppermute only.
A program may use at most 64 MiB of HBM per device.

```python
import jax
import jax.numpy as jnp
from jax import lax

DS = 768
DT = 1024
ROWS_DEV = 384
SPAN = 2
ROWS = 12288
N_GROUP = 2
N_MEMBER = 16


def draw_teacher(key, part):
    base = jnp.clip(jax.random.normal(jax.random.fold_in(key, 11), (ROWS, DT), jnp.float32), -6.0, 6.0)
    shared = jnp.clip(jax.random.normal(jax.random.fold_in(key, 12), (DT,), jnp.float32), -4.0, 4.0)
    position = jnp.arange(ROWS, dtype=jnp.float32) / ROWS
    strength = 0.35 * position
    values = base + strength[:, None] * shared[None, :]
    return jnp.clip(values, -14.0, 14.0).astype(jnp.bfloat16)


def draw_counts(key, part):
    position = jnp.arange(ROWS, dtype=jnp.int32)
    ceiling = 1 + 7 * position // ROWS
    return (1 + jax.random.randint(key, (ROWS,), 0, ceiling)).astype(jnp.int32)


def draw_plan(key, part):
    member_ids = jnp.arange(N_MEMBER, dtype=jnp.int32)
    chance = jnp.where(member_ids < N_MEMBER // 4, 95, 30)
    lower_cols = []
    upper_cols = []
    for offset in range(1, SPAN + 1):
        rolled = jax.random.randint(jax.random.fold_in(key, offset), (N_GROUP, N_MEMBER), 0, 100)
        edge = (rolled < chance[None, :]).astype(jnp.int32)
        upper_cols.append(edge)
        lower_cols.append(jnp.roll(edge, offset, axis=1))
    rolled = jax.random.randint(jax.random.fold_in(key, 977), (N_GROUP // 2, N_MEMBER), 0, 100)
    cross = jnp.repeat((rolled < chance[None, :]).astype(jnp.int32), 2, axis=0)
    return jnp.stack(lower_cols + upper_cols + [cross], axis=-1).astype(jnp.int32)


def block_scale(own_key, extent, shards, smallest, largest):
    loudness = 1.0
    for dim, blocks in shards:
        heights = jax.random.uniform(jax.random.fold_in(jax.random.fold_in(own_key, 6), dim), (blocks,), jnp.float32, smallest / len(shards), largest / len(shards))
        loudness = loudness * jnp.repeat(jnp.exp(heights), extent[dim] // blocks).reshape((-1,) + (1,) * (len(extent) - 1 - dim))
    return loudness


def noise(stream_key, shape, width, reach, split=(), kind=jnp.bfloat16):
    result = jax.random.normal(stream_key, shape, jnp.float32) * width
    if len(split) > 0:
        result = block_scale(stream_key, shape, split, -0.22, 0.18) * result
    return jnp.clip(result, min=-reach, max=reach).astype(kind)


def setup_inputs(seed: int = 0) -> dict:
    arg_keys = jax.random.split(jax.random.key(seed), 5)
    return {
        "student": noise(arg_keys[0], (ROWS, DS), 0.05, 0.29882812, ((0, 32),)),
        "teacher": draw_teacher(jax.random.fold_in(arg_keys[4], 71), 0),
        "counts": draw_counts(jax.random.fold_in(arg_keys[4], 71), 0),
        "plan": draw_plan(jax.random.fold_in(arg_keys[4], 71), 0),
    }


EPS = 1e-06

def normalize(embeddings):
    widened = embeddings.astype(jnp.float32)
    row_scale = lax.rsqrt(lax.optimization_barrier(jnp.sum(widened * widened, axis=-1, keepdims=True)) + EPS)
    return ((widened * row_scale).astype(jnp.bfloat16), row_scale)

def pair_terms(local_s, local_t, local_w, partner_s, partner_t, partner_w, switches):
    highest = lax.Precision.HIGHEST
    student_sim = jnp.einsum('bid,bjd->bij', local_s.astype(jnp.float32), partner_s.astype(jnp.float32), precision=highest)
    teacher_sim = jnp.einsum('bid,bjd->bij', local_t.astype(jnp.float32), partner_t.astype(jnp.float32), precision=highest)
    mismatch = student_sim - teacher_sim
    pair_weight = local_w[:, :, None] * partner_w[:, None, :] * switches[:, None, None]
    rounded = lax.optimization_barrier((pair_weight * mismatch).astype(jnp.bfloat16))
    coefficient = rounded.astype(jnp.float32)
    contrib = jnp.einsum('bij,bjd->bid', coefficient, partner_s.astype(jnp.float32), precision=highest)
    return (contrib, jnp.sum(pair_weight * mismatch * mismatch), jnp.sum(pair_weight))

def reference(student, teacher, counts, plan):
    unit_student, row_scale = normalize(student)
    unit_teacher, unused_scale = normalize(teacher)
    weights = counts.astype(jnp.float32)
    switches = plan.astype(jnp.float32)
    s_blocks = unit_student.reshape(N_GROUP, N_MEMBER, ROWS_DEV, DS)
    t_blocks = unit_teacher.reshape(N_GROUP, N_MEMBER, ROWS_DEV, DT)
    w_blocks = weights.reshape(N_GROUP, N_MEMBER, ROWS_DEV)
    scale_blocks = row_scale.reshape(N_GROUP, N_MEMBER, ROWS_DEV, 1)
    all_on = jnp.ones((N_MEMBER,), jnp.float32)
    loss_sum = jnp.float32(0.0)
    weight_sum = jnp.float32(0.0)
    gradients = []
    for group_index in range(N_GROUP):
        local_rows = (s_blocks[group_index], t_blocks[group_index], w_blocks[group_index])
        summed_grad, loss_part, weight_part = pair_terms(*local_rows, *local_rows, all_on)
        loss_sum = loss_sum + loss_part
        weight_sum = weight_sum + weight_part
        for offset in range(1, SPAN + 1):
            for column, moved in ((offset - 1, offset), (SPAN + offset - 1, -offset)):
                partner = tuple((jnp.roll(array, moved, axis=0) for array in local_rows))
                contrib, loss_part, weight_part = pair_terms(*local_rows, *partner, switches[group_index, :, column])
                summed_grad = summed_grad + contrib
                loss_sum = loss_sum + loss_part
                weight_sum = weight_sum + weight_part
        other = group_index ^ 1
        partner = (s_blocks[other], t_blocks[other], w_blocks[other])
        contrib, loss_part, weight_part = pair_terms(*local_rows, *partner, switches[group_index, :, 2 * SPAN])
        summed_grad = summed_grad + contrib
        loss_sum = loss_sum + loss_part
        weight_sum = weight_sum + weight_part
        unit_float = s_blocks[group_index].astype(jnp.float32)
        along_unit = lax.optimization_barrier(jnp.sum(summed_grad * unit_float, axis=-1, keepdims=True))
        gradients.append(4.0 * scale_blocks[group_index] * (summed_grad - along_unit * unit_float))
    grad_student = jnp.stack(gradients).reshape(ROWS, DS)
    loss = DS * loss_sum / weight_sum
    return (grad_student, loss)
```

```python
import functools

import jax
import jax.numpy as jnp
from jax import lax
from jax.experimental import pallas as pl
from jax.experimental.pallas import tpu as pltpu
from jax.sharding import PartitionSpec as P

EPS = 1e-06
AXES = ("group", "member")
F32 = jnp.float32
BF16 = jnp.bfloat16
OWN_NEAR, OWN_FAR, OWN_CROSS, OUTER_NEAR = range(4)


def units(raw):
    wide = raw.astype(F32)
    scale = lax.rsqrt(jnp.sum(wide * wide, axis=-1, keepdims=True) + EPS)
    return (wide * scale).astype(BF16), scale


def similarity(left, right):
    return lax.dot_general(left, right, (((1,), (1,)), ((), ())), preferred_element_type=F32)


def column(row):
    wide = jnp.broadcast_to(row, (128, row.shape[1]))
    return jnp.transpose(wide)[:, :1]


def lanes(values):
    row = jnp.sum(values, axis=0, keepdims=True)
    return sum(row[:, k : k + 128] for k in range(0, row.shape[1], 128))


def pair(left, right, weight_column, weight_row):
    mismatch = similarity(left[0], right[0]) - similarity(left[1], right[1])
    weight = weight_column * weight_row
    weighted = weight * mismatch
    return weighted.astype(BF16), lanes(weighted * mismatch), lanes(weight)


def tile(loss, weight):
    rows = lax.broadcasted_iota(jnp.int32, (8, 128), 0)
    zero = jnp.zeros((8, 128), F32)
    return jnp.where(rows == 0, loss, zero) + jnp.where(rows == 1, weight, zero)


def dot(left, right):
    return jnp.dot(left, right, preferred_element_type=F32)


def local_kernel(count, s, t, near_s, near_t, meta, near_meta, us, ut, near_us, near_ut, scale, total, sums):
    us[...], factor = units(s[...])
    ut[...], _ = units(t[...])
    near_us[...], _ = units(near_s[...])
    near_ut[...], _ = units(near_t[...])
    scale[...] = jnp.broadcast_to(factor, scale.shape)
    own_row = meta[:, :count]
    own = column(own_row)
    switch = meta[:, count + OWN_NEAR : count + OWN_NEAR + 1]
    here = (us[...], ut[...])
    coefficient, loss, weight = pair(here, here, own, own_row)
    total[...] = dot(coefficient, us[...])
    coefficient, loss_2, weight_2 = pair(here, (near_us[...], near_ut[...]), own, near_meta[:, :count] * switch)
    total[...] += dot(coefficient, near_us[...])
    sums[...] = tile(loss + loss_2, weight + weight_2)


def cross_kernel(count, us, ut, far_s, far_t, meta, far_meta, before, sums_before, total, sums):
    far_us, _ = units(far_s[...])
    far_ut, _ = units(far_t[...])
    switch = meta[:, count + OWN_CROSS : count + OWN_CROSS + 1]
    coefficient, loss, weight = pair(
        (us[...], ut[...]), (far_us, far_ut), column(meta[:, :count]), far_meta[:, :count] * switch
    )
    total[...] = before[...] + dot(coefficient, far_us)
    sums[...] = sums_before[...] + tile(loss, weight)


def ring_kernel(
    count, us, ut, near_us, near_ut, far_s, far_t, meta, near_meta, far_meta, before, sums_before,
    total, to_near, to_far, sums,
):
    far_us, _ = units(far_s[...])
    far_ut, _ = units(far_t[...])
    far = (far_us, far_ut)
    far_row = far_meta[:, :count]
    switch = meta[:, count + OWN_FAR : count + OWN_FAR + 1]
    coefficient, loss, weight = pair((us[...], ut[...]), far, column(meta[:, :count]), far_row * switch)
    total[...] = before[...] + dot(coefficient, far_us)
    to_far[...] = lax.dot_general(
        coefficient, us[...], (((0,), (0,)), ((), ())), preferred_element_type=F32
    ).astype(BF16)
    switch = near_meta[:, count + OUTER_NEAR : count + OUTER_NEAR + 1]
    coefficient, loss_2, weight_2 = pair(
        (near_us[...], near_ut[...]), far, column(near_meta[:, :count]), far_row * switch
    )
    to_near[...] = dot(coefficient, far_us).astype(BF16)
    sums[...] = sums_before[...] + tile(2.0 * loss + loss_2, 2.0 * weight + weight_2)


def final_kernel(us, scale, total, from_near, from_far, grad):
    unit = us[...].astype(F32)
    summed = total[...] + from_near[...].astype(F32) + from_far[...].astype(F32)
    along = jnp.sum(summed * unit, axis=-1, keepdims=True)
    grad[...] = 4.0 * scale[:, :1] * (summed - along * unit)


def call(kernel, outs, flops, *operands):
    size = sum(x.size * x.dtype.itemsize for x in operands)
    size += sum(x.size * x.dtype.itemsize for x in outs)
    return pl.pallas_call(
        kernel,
        out_shape=outs,
        compiler_params=pltpu.CompilerParams(vmem_limit_bytes=48 << 20),
        cost_estimate=pl.CostEstimate(flops=flops, bytes_accessed=size, transcendentals=0),
    )(*operands)


def per_device(student, teacher, counts, plan):
    groups, members = lax.axis_size("group"), lax.axis_size("member")
    rows, ds = student.shape
    dt = teacher.shape[1]

    def route(target):
        pairs = []
        for g in range(groups):
            for m in range(members):
                to_g, to_m = target(g, m)
                pairs.append((g * members + m, to_g * members + to_m % members))
        return functools.partial(lax.ppermute, axis_name=AXES, perm=pairs)

    to_ring = route(lambda g, m: (g, m - 2 + 4 * (m % 2)))
    back = route(lambda g, m: (g, m + 2 - 4 * (m % 2)))
    to_near = route(lambda g, m: (g, m ^ 1))
    to_cross = route(lambda g, m: (g ^ 1, m))

    odd = lax.axis_index("member") % 2
    switches = plan.reshape(-1).astype(F32)
    even_slots = jnp.stack([switches[i] for i in (2, 3, 4, 0)])
    odd_slots = jnp.stack([switches[i] for i in (0, 1, 4, 2)])
    slots = jnp.where(odd == 1, odd_slots, even_slots)
    meta = jnp.concatenate([counts.astype(F32), slots, jnp.zeros((124,), F32)]).reshape(1, rows + 128)

    ring_s, ring_t = to_ring(student), to_ring(teacher)
    cross_s, cross_t = to_cross(student), to_cross(teacher)
    near_s, near_t, near_meta = to_near(student), to_near(teacher), to_near(meta)
    ring_meta, cross_meta = to_ring(meta), to_cross(meta)

    f = jax.ShapeDtypeStruct
    sim = 2 * rows * rows * (ds + dt)
    mix = 2 * rows * rows * ds
    acc, sums_shape = f((rows, ds), F32), f((8, 128), F32)
    unit_s, unit_t = f((rows, ds), BF16), f((rows, dt), BF16)
    us, ut, near_us, near_ut, scale, total, sums = call(
        functools.partial(local_kernel, rows),
        (unit_s, unit_t, unit_s, unit_t, f((rows, 128), F32), acc, sums_shape),
        2 * (sim + mix),
        student, teacher, near_s, near_t, meta, near_meta,
    )
    total, sums = call(
        functools.partial(cross_kernel, rows),
        (acc, sums_shape),
        sim + mix,
        us, ut, cross_s, cross_t, meta, cross_meta, total, sums,
    )
    total, give_near, give_back, sums = call(
        functools.partial(ring_kernel, rows),
        (acc, unit_s, unit_s, sums_shape),
        2 * sim + 3 * mix,
        us, ut, near_us, near_ut, ring_s, ring_t, meta, near_meta, ring_meta, total, sums,
    )
    from_far = back(give_back)
    from_near = to_near(give_near)

    step = 1
    while step < members:
        sums = sums + route(lambda g, m: (g, m ^ step))(sums)
        step *= 2
    step = 1
    while step < groups:
        sums = sums + route(lambda g, m: (g ^ step, m))(sums)
        step *= 2
    loss = ds * jnp.sum(sums[0]) / jnp.sum(sums[1])

    (grad,) = call(final_kernel, (acc,), 0, us, scale, total, from_near, from_far)
    return grad, loss


def solution(mesh):
    return jax.shard_map(
        per_device,
        mesh=mesh,
        in_specs=(
            P(AXES, None),
            P(AXES, None),
            P(AXES),
            P("group", "member", None),
        ),
        out_specs=(P(AXES, None), P()),
        check_vma=False,
    )
```

```python
import functools

import jax
import jax.numpy as jnp
from jax import lax
from jax.experimental import pallas as pl
from jax.experimental.pallas import tpu as pltpu
from jax.sharding import PartitionSpec as P

EPS = 1e-06
AXES = ("group", "member")
F32 = jnp.float32
BF16 = jnp.bfloat16
META, RING_META = 8, 16
PIECES = 4


def units(raw):
    wide = raw.astype(F32)
    scale = lax.rsqrt(jnp.sum(wide * wide, axis=-1, keepdims=True) + EPS)
    return (wide * scale).astype(BF16), scale


def similarity(left, right):
    return lax.dot_general(left, right, (((1,), (1,)), ((), ())), preferred_element_type=F32)


def dot(left, right):
    return jnp.dot(left, right, preferred_element_type=F32)


def dot_transposed(left, right):
    return lax.dot_general(left, right, (((0,), (0,)), ((), ())), preferred_element_type=F32)


def column(row):
    wide = jnp.broadcast_to(row, (128, row.shape[1]))
    return jnp.transpose(wide)[:, :1]


def lanes(values):
    row = jnp.sum(values, axis=0, keepdims=True)
    return sum(row[:, k : k + 128] for k in range(0, row.shape[1], 128))


def weigh(mismatch, weight_column, weight_row):
    weight = weight_column * weight_row
    weighted = weight * mismatch
    return weighted.astype(BF16), lanes(weighted * mismatch), lanes(weight)


def tile(loss, weight):
    rows = lax.broadcasted_iota(jnp.int32, (8, 128), 0)
    zero = jnp.zeros((8, 128), F32)
    return jnp.where(rows == 0, loss, zero) + jnp.where(rows == 1, weight, zero)


class Packed:
    def __init__(self, ref, rows, ds):
        self.ref, self.rows, self.ds = ref, rows, ds

    @property
    def s(self):
        return self.ref[: self.rows, : self.ds]

    @property
    def t(self):
        return self.ref[: self.rows, self.ds :]

    def meta(self):
        return self.ref[self.rows :, : self.ds].astype(F32)

    def counts(self):
        return self.meta()[0:1, : self.rows]

    def switch(self, if_even, if_odd):
        odd = lax.axis_index("member") % 2 == 1
        plan = self.meta()[1:2, :128]
        return jnp.where(odd, plan[:, if_odd : if_odd + 1], plan[:, if_even : if_even + 1])


def pack_kernel(counts_hbm, plan_hbm, s_hbm, t_hbm, both, ring, scale, counts, plan, s, t, arrived):
    rows, ds = s.shape
    pieces = [pl.ds(i * (rows // PIECES), rows // PIECES) for i in range(PIECES)]
    copies = [
        pltpu.make_async_copy(source.at[piece], target.at[piece], arrived.at[i, k])
        for i, piece in enumerate(pieces)
        for k, (source, target) in enumerate(((s_hbm, s), (t_hbm, t)))
    ]
    small = [
        pltpu.make_async_copy(source, target, arrived.at[PIECES, k])
        for k, (source, target) in enumerate(((counts_hbm, counts), (plan_hbm, plan)))
    ]
    for copy in copies + small:
        copy.start()
    for i, piece in enumerate(pieces):
        copies[2 * i].wait()
        unit, factor = units(s[piece])
        scale[piece] = jnp.broadcast_to(factor, (rows // PIECES, 128))
        both[piece, :ds] = unit
        ring[piece, :ds] = unit
        copies[2 * i + 1].wait()
        unit, _ = units(t[piece])
        both[piece, ds:] = unit
        ring[piece, ds:] = unit

    def widen(values):
        return jnp.concatenate([values, jnp.zeros((1, ds - values.shape[1]), F32)], axis=1)

    for copy in small:
        copy.wait()
    at = lax.broadcasted_iota(jnp.int32, (RING_META, ds), 0)
    meta = jnp.where(at == 0, widen(counts[...].astype(F32).reshape(1, rows)), 0.0)
    meta = jnp.where(at == 1, widen(plan[...].astype(F32)), meta).astype(BF16)
    both[rows:, :ds] = meta[:META]
    ring[rows:, :ds] = meta
    both[rows:, ds:] = jnp.zeros((META, t.shape[1]), BF16)
    ring[rows:, ds:] = jnp.zeros((RING_META, t.shape[1]), BF16)


def local_kernel(rows, ds, own, near, total, sums):
    own, near = Packed(own, rows, ds), Packed(near, rows, ds)
    own_column = column(own.counts())
    mismatch = similarity(own.s, own.s) - similarity(own.t, own.t)
    coefficient, loss, weight = weigh(mismatch, own_column, own.counts())
    total[...] = dot(coefficient, own.s)
    mismatch = similarity(own.s, near.s) - similarity(own.t, near.t)
    coefficient, loss_2, weight_2 = weigh(mismatch, own_column, near.counts() * own.switch(2, 0))
    total[...] += dot(coefficient, near.s)
    sums[...] = tile(loss + loss_2, weight + weight_2)


def cross_kernel(rows, ds, own, far, before, sums_before, total, give, sums):
    own, far = Packed(own, rows, ds), Packed(far, rows, ds)
    mismatch = similarity(own.s, far.s) - similarity(own.t, far.t)
    coefficient, loss, weight = weigh(mismatch, column(own.counts()), far.counts() * own.switch(4, 4))
    give[...] = dot_transposed(coefficient, own.s).astype(BF16)
    total[...] = before[...] + dot(coefficient, far.s)
    sums[...] = sums_before[...] + tile(2.0 * loss, 2.0 * weight)


def ring_kernel(rows, ds, own, near, far, coefficients, near_coefficients, sums):
    own, near, far = Packed(own, rows, ds), Packed(near, rows, ds), Packed(far, rows, ds)
    mismatch = similarity(own.s, far.s) - similarity(own.t, far.t)
    coefficients[...], loss, weight = weigh(mismatch, column(own.counts()), far.counts() * own.switch(3, 1))
    mismatch = similarity(near.s, far.s) - similarity(near.t, far.t)
    near_coefficients[...], loss_2, weight_2 = weigh(
        mismatch, column(near.counts()), far.counts() * near.switch(2, 0)
    )
    sums[...] = tile(2.0 * loss + loss_2, 2.0 * weight + weight_2)


def ring_mix_kernel(rows, ds, own, far, coefficients, near_coefficients, total, to_near, to_far):
    own, far = Packed(own, rows, ds), Packed(far, rows, ds)
    to_far[...] = dot_transposed(coefficients[...], own.s).astype(BF16)
    to_near[...] = dot(near_coefficients[...], far.s).astype(BF16)
    total[...] = dot(coefficients[...], far.s)


def final_kernel(rows, ds, own, scale, total, ring_total, from_near, from_far, from_cross, grad):
    unit = Packed(own, rows, ds).s.astype(F32)
    received = from_near[...].astype(F32) + from_far[...].astype(F32) + from_cross[...].astype(F32)
    summed = total[...] + ring_total[...] + received
    along = jnp.sum(summed * unit, axis=-1, keepdims=True)
    grad[...] = 4.0 * scale[:, :1] * (summed - along * unit)


def loss_kernel(width, sums, loss):
    total = jnp.sum(sums[...], axis=1, keepdims=True)
    loss[...] = width * total[0:1] / total[1:2]


def call(kernel, outs, vmem_mib, *operands, flops=0, **options):
    return pl.pallas_call(
        kernel,
        out_shape=outs,
        compiler_params=pltpu.CompilerParams(vmem_limit_bytes=vmem_mib << 20),
        cost_estimate=pl.CostEstimate(flops=flops, bytes_accessed=0, transcendentals=0),
        **options,
    )(*operands)


def powers(first, end):
    return [first << i for i in range(end.bit_length()) if first << i < end]


def per_device(student, teacher, counts, plan):
    groups, members = lax.axis_size("group"), lax.axis_size("member")
    rows, ds = student.shape
    dt = teacher.shape[1]

    def route(target):
        pairs = []
        for g in range(groups):
            for m in range(members):
                to_g, to_m = target(g, m)
                if to_g is not None:
                    pairs.append((g * members + m, to_g * members + to_m % members))
        return functools.partial(lax.ppermute, axis_name=AXES, perm=pairs)

    to_ring = route(lambda g, m: (g, m - 2 + 4 * (m % 2)))
    ring_back = route(lambda g, m: (g, m + 2 - 4 * (m % 2)))
    to_near = route(lambda g, m: (g, m ^ 1))
    to_cross = route(lambda g, m: (g ^ 1 if (g + m) % 2 == 0 else None, m))
    cross_back = route(lambda g, m: (g ^ 1 if (g + m) % 2 == 1 else None, m))

    f = jax.ShapeDtypeStruct
    acc, half, sums_shape = f((rows, ds), F32), f((rows, ds), BF16), f((8, 128), F32)

    def on_blocks(kernel):
        return functools.partial(kernel, rows, ds)

    own, own_ring, scale = call(
        pack_kernel,
        (f((rows + META, ds + dt), BF16), f((rows + RING_META, ds + dt), BF16), f((rows, 128), F32)),
        24,
        *(pltpu.with_memory_space_constraint(x, pltpu.HBM) for x in (counts, plan.reshape(1, -1), student, teacher)),
        in_specs=[pl.BlockSpec(memory_space=pltpu.HBM)] * 4,
        scratch_shapes=[
            pltpu.VMEM((rows,), jnp.int32),
            pltpu.VMEM((1, plan.size), jnp.int32),
            pltpu.VMEM((rows, ds), BF16),
            pltpu.VMEM((rows, dt), BF16),
            pltpu.SemaphoreType.DMA((PIECES + 1, 2)),
        ],
    )
    near, cross, ring = to_near(own), to_cross(own), to_ring(own_ring)

    total, sums = call(on_blocks(local_kernel), (acc, sums_shape), 24, own, near)
    total, give_cross, sums = call(
        on_blocks(cross_kernel), (acc, half, sums_shape), 24, own, cross, total, sums
    )
    from_cross = cross_back(give_cross)
    pair_shape = f((rows, rows), BF16)
    coefficients, near_coefficients, ring_sums = call(
        on_blocks(ring_kernel), (pair_shape, pair_shape, sums_shape), 24, own, near, ring, flops=10**10
    )
    ring_total, give_near, give_ring = call(
        on_blocks(ring_mix_kernel), (acc, half, half), 24, own, ring, coefficients, near_coefficients, flops=10**9
    )

    sums = sums + ring_sums
    sums = sums + to_near(sums)
    sums, from_cross, give_near, give_ring = lax.optimization_barrier((sums, from_cross, give_near, give_ring))
    from_near = to_near(give_near)
    from_ring = ring_back(give_ring)
    routes = [route(lambda g, m, bit=bit: (g ^ bit, m)) for bit in powers(1, groups)]
    routes += [route(lambda g, m, bit=bit: (g, m ^ bit)) for bit in reversed(powers(2, members))]
    for exchange in routes[:-1]:
        sums = sums + exchange(sums)
    received = routes[-1](sums)

    (grad,) = call(
        on_blocks(final_kernel), (acc,), 24, own, scale, total, ring_total, from_near, from_ring, from_cross
    )
    sums, grad = lax.optimization_barrier((sums, grad))
    (loss,) = call(functools.partial(loss_kernel, ds), (f((1, 1), F32),), 24, sums + received)
    return grad, loss.reshape(())


def solution(mesh):
    return jax.shard_map(
        per_device,
        mesh=mesh,
        in_specs=(
            P(AXES, None),
            P(AXES, None),
            P(AXES),
            P("group", "member", None),
        ),
        out_specs=(P(AXES, None), P()),
        check_vma=False,
    )
```

```python
import functools

import jax
import jax.numpy as jnp
from jax import lax
from jax.experimental import pallas as pl
from jax.experimental.pallas import tpu as pltpu
from jax.sharding import PartitionSpec as P

EPS = 1e-06
AXES = ("group", "member")
F32 = jnp.float32
BF16 = jnp.bfloat16
META = 16
PIECES = 3


def units(raw):
    wide = raw.astype(F32)
    scale = lax.rsqrt(jnp.sum(wide * wide, axis=-1, keepdims=True) + EPS)
    return (wide * scale).astype(BF16), scale


def similarity(left, right):
    return lax.dot_general(left, right, (((1,), (1,)), ((), ())), preferred_element_type=F32)


def dot(left, right):
    return jnp.dot(left, right, preferred_element_type=F32)


def dot_transposed(left, right):
    return lax.dot_general(left, right, (((0,), (0,)), ((), ())), preferred_element_type=F32)


def column(row):
    wide = jnp.broadcast_to(row, (128, row.shape[1]))
    return jnp.transpose(wide)[:, :1]


def lanes(values):
    row = jnp.sum(values, axis=0, keepdims=True)
    return sum(row[:, k : k + 128] for k in range(0, row.shape[1], 128))


def weigh(mismatch, weight_column, weight_row, twice=0):
    weight = weight_column * weight_row
    weighted = weight * mismatch
    loss = weighted * mismatch
    sums = [lanes(loss) + lanes(loss[:, :twice]), lanes(weight) + lanes(weight[:, :twice])] if twice else [lanes(loss), lanes(weight)]
    return weighted.astype(BF16), *sums


def tile(loss, weight):
    rows = lax.broadcasted_iota(jnp.int32, (8, 128), 0)
    zero = jnp.zeros((8, 128), F32)
    return jnp.where(rows == 0, loss, zero) + jnp.where(rows == 1, weight, zero)


class Packed:
    def __init__(self, student, teacher, rows):
        self.student, self.teacher, self.rows = student, teacher, rows

    @property
    def s(self):
        return self.student[: self.rows]

    @property
    def t(self):
        return self.teacher[...]

    def counts(self):
        return self.student[self.rows :].astype(F32)[0:1, : self.rows]

    def switch(self, if_even, if_odd):
        odd = lax.axis_index("member") % 2 == 1
        plan = self.student[self.rows :].astype(F32)[1:2, :128]
        return jnp.where(odd, plan[:, if_odd : if_odd + 1], plan[:, if_even : if_even + 1])


def pack_kernel(counts_hbm, plan_hbm, s_hbm, t_hbm, both, student, teacher, scale, counts, plan, s, t, arrived):
    rows, ds = s.shape
    copies = [
        pltpu.make_async_copy(source, target, arrived.at[i])
        for i, (source, target) in enumerate(((s_hbm, s), (t_hbm, t), (counts_hbm, counts), (plan_hbm, plan)))
    ]
    for copy in copies:
        copy.start()
    copies[0].wait()
    unit, factor = units(s[...])
    scale[...] = jnp.broadcast_to(factor, scale.shape)
    both[:, :ds] = unit
    student[:rows] = unit
    copies[1].wait()
    unit, _ = units(t[...])
    both[:, ds:] = unit
    teacher[...] = unit

    def widen(values):
        return jnp.concatenate([values, jnp.zeros((1, ds - values.shape[1]), F32)], axis=1)

    copies[2].wait()
    copies[3].wait()
    at = lax.broadcasted_iota(jnp.int32, (META, ds), 0)
    meta = jnp.where(at == 0, widen(counts[...].astype(F32).reshape(1, rows)), 0.0)
    student[rows:] = jnp.where(at == 1, widen(plan[...].astype(F32)), meta).astype(BF16)


def local_kernel(rows, both, own_s, own_t, near_s, near_t, mates, total, sums):
    own, near = Packed(own_s, own_t, rows), Packed(near_s, near_t, rows)
    mates[:rows] = both[...]
    mates[rows:] = jnp.concatenate([near.s, near.t], axis=1)
    own_column = column(own.counts())
    mismatch = similarity(own.s, own.s) - similarity(own.t, own.t)
    coefficient, loss, weight = weigh(mismatch, own_column, own.counts())
    total[...] = dot(coefficient, own.s)
    mismatch = similarity(own.s, near.s) - similarity(own.t, near.t)
    coefficient, loss_2, weight_2 = weigh(mismatch, own_column, near.counts() * own.switch(2, 0))
    total[...] += dot(coefficient, near.s)
    sums[...] = tile(loss + loss_2, weight + weight_2)


def cross_kernel(rows, own_s, own_t, far_s, far_t, before, sums_before, total, give, sums):
    own, far = Packed(own_s, own_t, rows), Packed(far_s, far_t, rows)
    mismatch = similarity(own.s, far.s) - similarity(own.t, far.t)
    coefficient, loss, weight = weigh(mismatch, column(own.counts()), far.counts() * own.switch(4, 4))
    give[...] = dot_transposed(coefficient, own.s).astype(BF16)
    total[...] = before[...] + dot(coefficient, far.s)
    sums[...] = sums_before[...] + tile(2.0 * loss, 2.0 * weight)


def ring_kernel(rows, own_s, near_s, mates, far, far_counts, sums_before, coefficients, to_far, sums):
    own, near, ds = Packed(own_s, None, rows), Packed(near_s, None, rows), own_s.shape[1]
    mismatch = similarity(far[:, :ds], mates[:, :ds]) - similarity(far[:, ds:], mates[:, ds:])
    mates_row = jnp.concatenate([own.counts() * own.switch(3, 1), near.counts() * near.switch(2, 0)], axis=1)
    far_column = column(far_counts[...].astype(F32).reshape(1, rows))
    coefficients[...], loss, weight = weigh(mismatch, far_column, mates_row, twice=rows)
    to_far[...] = dot(coefficients[:, :rows], own.s).astype(BF16)
    sums[...] = sums_before[...] + tile(loss, weight)


def ring_mix_kernel(rows, far, coefficients, before, total, to_near):
    far_s = far[:, : before.shape[1]]
    to_near[...] = dot_transposed(coefficients[:, rows:], far_s).astype(BF16)
    total[...] = before[...] + dot_transposed(coefficients[:, :rows], far_s)


def final_kernel(rows, own, scale, total, from_near, from_far, from_cross, grad, result, sent):
    size = rows // PIECES
    copies = []
    for i in range(PIECES):
        piece = pl.ds(i * size, size)
        unit = own[piece].astype(F32)
        received = from_near[piece].astype(F32) + from_far[piece].astype(F32) + from_cross[piece].astype(F32)
        summed = total[piece] + received
        along = jnp.sum(summed * unit, axis=-1, keepdims=True)
        result[piece] = 4.0 * scale[piece, :1] * (summed - along * unit)
        copies.append(pltpu.make_async_copy(result.at[piece], grad.at[piece], sent.at[i]))
        copies[-1].start()
    for copy in copies:
        copy.wait()


def loss_kernel(width, sums, loss):
    total = jnp.sum(sums[...], axis=1, keepdims=True)
    loss[...] = width * total[0:1] / total[1:2]


def call(kernel, outs, vmem_mib, *operands, flops=0, **options):
    return pl.pallas_call(
        kernel,
        out_shape=outs,
        compiler_params=pltpu.CompilerParams(vmem_limit_bytes=vmem_mib << 20),
        cost_estimate=pl.CostEstimate(flops=flops, bytes_accessed=0, transcendentals=0),
        **options,
    )(*operands)


def powers(first, end):
    return [first << i for i in range(end.bit_length()) if first << i < end]


def per_device(student, teacher, counts, plan):
    groups, members = lax.axis_size("group"), lax.axis_size("member")
    rows, ds = student.shape
    dt = teacher.shape[1]

    def route(target):
        pairs = []
        for g in range(groups):
            for m in range(members):
                to_g, to_m = target(g, m)
                if to_g is not None:
                    pairs.append((g * members + m, to_g * members + to_m % members))
        return functools.partial(lax.ppermute, axis_name=AXES, perm=pairs)

    to_ring = route(lambda g, m: (g, m - 2 + 4 * (m % 2)))
    ring_back = route(lambda g, m: (g, m + 2 - 4 * (m % 2)))
    to_near = route(lambda g, m: (g, m ^ 1))
    to_cross = route(lambda g, m: (g ^ 1 if (g + m) % 2 == 0 else None, m))
    cross_back = route(lambda g, m: (g ^ 1 if (g + m) % 2 == 1 else None, m))

    f = jax.ShapeDtypeStruct
    acc, half, sums_shape = f((rows, ds), F32), f((rows, ds), BF16), f((8, 128), F32)

    def on_blocks(kernel):
        return functools.partial(kernel, rows)

    both, own_s, own_t, scale = call(
        pack_kernel,
        (f((rows, ds + dt), BF16), f((rows + META, ds), BF16), f((rows, dt), BF16), f((rows, 128), F32)),
        24,
        *(pltpu.with_memory_space_constraint(x, pltpu.HBM) for x in (counts, plan.reshape(1, -1), student, teacher)),
        in_specs=[pl.BlockSpec(memory_space=pltpu.HBM)] * 4,
        scratch_shapes=[
            pltpu.VMEM((rows,), jnp.int32),
            pltpu.VMEM((1, plan.size), jnp.int32),
            pltpu.VMEM((rows, ds), BF16),
            pltpu.VMEM((rows, dt), BF16),
            pltpu.SemaphoreType.DMA((4,)),
        ],
    )
    ring, ring_counts = to_ring(both), to_ring(counts)
    near, cross = (to_near(own_s), to_near(own_t)), (to_cross(own_s), to_cross(own_t))

    mates, total, sums = call(
        on_blocks(local_kernel), (f((2 * rows, ds + dt), BF16), acc, sums_shape), 24, both, own_s, own_t, *near
    )
    total, give_cross, sums = call(
        on_blocks(cross_kernel), (acc, half, sums_shape), 24, own_s, own_t, *cross, total, sums
    )
    from_cross = cross_back(give_cross)
    coefficients, give_ring, sums = call(
        on_blocks(ring_kernel), (f((rows, 2 * rows), BF16), half, sums_shape), 24,
        own_s, near[0], mates, ring, ring_counts, sums,
        flops=10**10,
    )
    total, give_near = call(on_blocks(ring_mix_kernel), (acc, half), 24, ring, coefficients, total)
    from_ring = ring_back(give_ring)
    across = [route(lambda g, m, bit=bit: (g ^ bit, m)) for bit in powers(1, groups)]
    along = [route(lambda g, m, bit=bit: (g, m ^ bit)) for bit in powers(2, members)]
    sums = sums + along[0](sums)
    sums, from_cross, give_near = lax.optimization_barrier((sums, from_cross, give_near))
    from_near = to_near(give_near)
    for exchange in [to_near] + across + along[:1:-1]:
        sums = sums + exchange(sums)
    received = along[1](sums)

    (grad,) = call(
        on_blocks(final_kernel), (acc,), 24, own_s, scale, total, from_near, from_ring, from_cross,
        out_specs=(pl.BlockSpec(memory_space=pltpu.HBM),),
        scratch_shapes=[pltpu.VMEM((rows, ds), F32), pltpu.SemaphoreType.DMA((PIECES,))],
    )
    sums, grad = lax.optimization_barrier((sums, grad))
    (loss,) = call(functools.partial(loss_kernel, ds), (f((1, 1), F32),), 24, sums + received)
    return grad, loss.reshape(())


def solution(mesh):
    return jax.shard_map(
        per_device,
        mesh=mesh,
        in_specs=(
            P(AXES, None),
            P(AXES, None),
            P(AXES),
            P("group", "member", None),
        ),
        out_specs=(P(AXES, None), P()),
        check_vma=False,
    )
```

```python
import functools

import jax
import jax.numpy as jnp
from jax import lax
from jax.experimental import pallas as pl
from jax.experimental.pallas import tpu as pltpu
from jax.sharding import PartitionSpec as P

EPS = 1e-06
AXES = ("group", "member")
F32 = jnp.float32
BF16 = jnp.bfloat16
META = 16
PIECES = 3


def units(raw):
    wide = raw.astype(F32)
    scale = lax.rsqrt(jnp.sum(wide * wide, axis=-1, keepdims=True) + EPS)
    return (wide * scale).astype(BF16), scale


def similarity(left, right):
    return lax.dot_general(left, right, (((1,), (1,)), ((), ())), preferred_element_type=F32)


def dot(left, right):
    return jnp.dot(left, right, preferred_element_type=F32)


def dot_transposed(left, right):
    return lax.dot_general(left, right, (((0,), (0,)), ((), ())), preferred_element_type=F32)


def column(row):
    wide = jnp.broadcast_to(row, (128, row.shape[1]))
    return jnp.transpose(wide)[:, :1]


def lanes(values):
    row = jnp.sum(values, axis=0, keepdims=True)
    return sum(row[:, k : k + 128] for k in range(0, row.shape[1], 128))


def weigh(mismatch, weight_column, weight_row, twice=0):
    weight = weight_column * weight_row
    weighted = weight * mismatch
    loss = weighted * mismatch
    sums = [lanes(loss) + lanes(loss[:, :twice]), lanes(weight) + lanes(weight[:, :twice])] if twice else [lanes(loss), lanes(weight)]
    return weighted.astype(BF16), *sums


def tile(loss, weight):
    rows = lax.broadcasted_iota(jnp.int32, (8, 128), 0)
    zero = jnp.zeros((8, 128), F32)
    return jnp.where(rows == 0, loss, zero) + jnp.where(rows == 1, weight, zero)


class Packed:
    def __init__(self, first, second, rows, ds):
        self.first, self.second, self.rows, self.ds = first, second, rows, ds

    @property
    def s(self):
        return self.first[: self.rows, : self.ds]

    @property
    def t(self):
        return jnp.concatenate([self.first[: self.rows, self.ds :], self.second[...]], axis=1)

    def meta(self):
        return self.first[self.rows :, : self.ds].astype(F32)

    def counts(self, count=None):
        return self.meta()[0:1, : count or self.rows]

    def switch(self, if_even, if_odd):
        odd = lax.axis_index("member") % 2 == 1
        plan = self.meta()[1:2, :128]
        return jnp.where(odd, plan[:, if_odd : if_odd + 1], plan[:, if_even : if_even + 1])


def pack_kernel(counts_hbm, plan_hbm, s_hbm, t_hbm, both, first, second, student, numbers, scale, counts, plan, s, t, arrived):
    rows, ds = s.shape
    more = first.shape[1] - ds
    copies = [
        pltpu.make_async_copy(source, target, arrived.at[i])
        for i, (source, target) in enumerate(((s_hbm, s), (t_hbm, t), (counts_hbm, counts), (plan_hbm, plan)))
    ]
    for copy in copies:
        copy.start()
    copies[0].wait()
    unit, factor = units(s[...])
    scale[...] = jnp.broadcast_to(factor, scale.shape)
    student[...] = unit
    both[:, :ds] = unit
    first[:rows, :ds] = unit
    copies[1].wait()
    unit, _ = units(t[...])
    both[:, ds:] = unit
    first[:rows, ds:] = unit[:, :more]
    second[...] = unit[:, more:]

    def widen(values):
        return jnp.concatenate([values, jnp.zeros((1, first.shape[1] - values.shape[1]), F32)], axis=1)

    copies[2].wait()
    copies[3].wait()
    at = lax.broadcasted_iota(jnp.int32, (META, first.shape[1]), 0)
    meta = jnp.where(at == 0, widen(counts[...].astype(F32).reshape(1, rows)), 0.0)
    first[rows:] = jnp.where(at == 1, widen(plan[...].astype(F32)), meta).astype(BF16)
    numbers[...] = first[rows:, :ds]


def local_kernel(rows, ds, both, first, near_meta, near_student, near_teacher, mates, total, sums):
    own, near = Packed(first, None, rows, ds), Packed(near_meta, None, 0, ds)
    mates[:rows] = both[...]
    mates[rows:, :ds], _ = units(near_student[...])
    mates[rows:, ds:], _ = units(near_teacher[...])
    own_s, own_t, near_s, near_t = mates[:rows, :ds], mates[:rows, ds:], mates[rows:, :ds], mates[rows:, ds:]
    own_column = column(own.counts())
    mismatch = similarity(own_s, own_s) - similarity(own_t, own_t)
    coefficient, loss, weight = weigh(mismatch, own_column, own.counts())
    total[...] = dot(coefficient, own_s)
    mismatch = similarity(own_s, near_s) - similarity(own_t, near_t)
    coefficient, loss_2, weight_2 = weigh(mismatch, own_column, near.counts(rows) * own.switch(2, 0))
    total[...] += dot(coefficient, near_s)
    sums[...] = tile(loss + loss_2, weight + weight_2)


def cross_kernel(rows, ds, both, first, far_first, far_second, before, sums_before, total, give, sums):
    own, far = Packed(first, None, rows, ds), Packed(far_first, far_second, rows, ds)
    mismatch = similarity(both[:, :ds], far.s) - similarity(both[:, ds:], far.t)
    coefficient, loss, weight = weigh(mismatch, column(own.counts()), far.counts() * own.switch(4, 4))
    give[...] = dot_transposed(coefficient, both[:, :ds]).astype(BF16)
    total[...] = before[...] + dot(coefficient, far.s)
    sums[...] = sums_before[...] + tile(2.0 * loss, 2.0 * weight)


def ring_teacher_kernel(ds, mates, far, teacher_sim):
    unit, _ = units(far[...])
    teacher_sim[...] = similarity(unit, mates[:, ds:])


def ring_kernel(
    rows, ds, first, near_meta, mates, teacher_sim, far_s, far_counts, sums_before, coefficients, to_far, sums
):
    own, near = Packed(first, None, rows, ds), Packed(near_meta, None, 0, ds)
    mismatch = similarity(far_s[...], mates[:, :ds]) - teacher_sim[...]
    mates_row = jnp.concatenate([own.counts() * own.switch(3, 1), near.counts(rows) * near.switch(2, 0)], axis=1)
    far_column = column(far_counts[...].astype(F32).reshape(1, rows))
    coefficients[...], loss, weight = weigh(mismatch, far_column, mates_row, twice=rows)
    to_far[...] = dot(coefficients[:, :rows], mates[:rows, :ds]).astype(BF16)
    sums[...] = sums_before[...] + tile(loss, weight)


def ring_mix_kernel(rows, ds, far_s, coefficients, before, total, to_near):
    to_near[...] = dot_transposed(coefficients[:, rows:], far_s[...]).astype(BF16)
    total[...] = before[...] + dot_transposed(coefficients[:, :rows], far_s[...])


def final_kernel(rows, ds, own, scale, total, from_near, from_far, from_cross, grad, result, sent):
    size = rows // PIECES
    copies = []
    for i in range(PIECES):
        piece = pl.ds(i * size, size)
        unit = own[piece].astype(F32)
        received = from_near[piece].astype(F32) + from_far[piece].astype(F32) + from_cross[piece].astype(F32)
        summed = total[piece] + received
        along = jnp.sum(summed * unit, axis=-1, keepdims=True)
        result[piece] = 4.0 * scale[piece, :1] * (summed - along * unit)
        copies.append(pltpu.make_async_copy(result.at[piece], grad.at[piece], sent.at[i]))
        copies[-1].start()
    for copy in copies:
        copy.wait()


def loss_kernel(width, sums, loss):
    total = jnp.sum(sums[...], axis=1, keepdims=True)
    loss[...] = width * total[0:1] / total[1:2]


def call(kernel, outs, vmem_mib, *operands, flops=0, **options):
    return pl.pallas_call(
        kernel,
        out_shape=outs,
        compiler_params=pltpu.CompilerParams(vmem_limit_bytes=vmem_mib << 20),
        cost_estimate=pl.CostEstimate(flops=flops, bytes_accessed=0, transcendentals=0),
        **options,
    )(*operands)


def powers(first, end):
    return [first << i for i in range(end.bit_length()) if first << i < end]


def per_device(student, teacher, counts, plan):
    groups, members = lax.axis_size("group"), lax.axis_size("member")
    rows, ds = student.shape
    dt = teacher.shape[1]

    def route(target):
        pairs = []
        for g in range(groups):
            for m in range(members):
                to_g, to_m = target(g, m)
                if to_g is not None:
                    pairs.append((g * members + m, to_g * members + to_m % members))
        return functools.partial(lax.ppermute, axis_name=AXES, perm=pairs)

    to_ring = route(lambda g, m: (g, m - 2 + 4 * (m % 2)))
    ring_back = route(lambda g, m: (g, m + 2 - 4 * (m % 2)))
    to_near = route(lambda g, m: (g, m ^ 1))
    to_cross = route(lambda g, m: (g ^ 1 if (g + m) % 2 == 0 else None, m))
    cross_back = route(lambda g, m: (g ^ 1 if (g + m) % 2 == 1 else None, m))

    f = jax.ShapeDtypeStruct
    acc, half, sums_shape = f((rows, ds), F32), f((rows, ds), BF16), f((8, 128), F32)

    def on_blocks(kernel):
        return functools.partial(kernel, rows, ds)

    ring_t, near_t, near_s = to_ring(teacher), to_near(teacher), to_near(student)
    width = (ds + dt) // 2
    both, first, second, own_s, own_meta, scale = call(
        pack_kernel,
        (
            f((rows, ds + dt), BF16), f((rows + META, width), BF16), f((rows, ds + dt - width), BF16),
            f((rows, ds), BF16), f((META, ds), BF16), f((rows, 128), F32),
        ),
        24,
        *(pltpu.with_memory_space_constraint(x, pltpu.HBM) for x in (counts, plan.reshape(1, -1), student, teacher)),
        in_specs=[pl.BlockSpec(memory_space=pltpu.HBM)] * 4,
        scratch_shapes=[
            pltpu.VMEM((rows,), jnp.int32),
            pltpu.VMEM((1, plan.size), jnp.int32),
            pltpu.VMEM((rows, ds), BF16),
            pltpu.VMEM((rows, dt), BF16),
            pltpu.SemaphoreType.DMA((4,)),
        ],
    )
    ring_s, ring_counts = to_ring(own_s), to_ring(counts)
    near_meta, cross = to_near(own_meta), (to_cross(first), to_cross(second))

    mates, total, sums = call(
        on_blocks(local_kernel), (f((2 * rows, ds + dt), BF16), acc, sums_shape), 24, both, first, near_meta, near_s, near_t
    )
    total, give_cross, sums = call(
        on_blocks(cross_kernel), (acc, half, sums_shape), 24, both, first, *cross, total, sums
    )
    from_cross = cross_back(give_cross)
    (teacher_sim,) = call(
        functools.partial(ring_teacher_kernel, ds), (f((rows, 2 * rows), F32),), 24, mates, ring_t
    )
    coefficients, give_ring, sums = call(
        on_blocks(ring_kernel), (f((rows, 2 * rows), BF16), half, sums_shape), 24,
        first, near_meta, mates, teacher_sim, ring_s, ring_counts, sums,
        flops=10**10,
    )
    total, give_near = call(on_blocks(ring_mix_kernel), (acc, half), 24, ring_s, coefficients, total)
    from_ring = ring_back(give_ring)
    across = [route(lambda g, m, bit=bit: (g ^ bit, m)) for bit in powers(1, groups)]
    along = [route(lambda g, m, bit=bit: (g, m ^ bit)) for bit in powers(2, members)]
    sums = sums + along[0](sums)
    sums, give_near = lax.optimization_barrier((sums, give_near))
    from_near = to_near(give_near)
    sums = sums + to_near(sums)
    for exchange in across:
        sums = sums + exchange(sums)
    sums, from_cross = lax.optimization_barrier((sums, from_cross))
    for exchange in along[:1:-1]:
        sums = sums + exchange(sums)
    received = along[1](sums)

    (grad,) = call(
        on_blocks(final_kernel), (acc,), 24, own_s, scale, total, from_near, from_ring, from_cross,
        out_specs=(pl.BlockSpec(memory_space=pltpu.HBM),),
        scratch_shapes=[pltpu.VMEM((rows, ds), F32), pltpu.SemaphoreType.DMA((PIECES,))],
    )
    sums, grad = lax.optimization_barrier((sums, grad))
    (loss,) = call(functools.partial(loss_kernel, ds), (f((1, 1), F32),), 24, sums + received)
    return grad, loss.reshape(())


def solution(mesh):
    return jax.shard_map(
        per_device,
        mesh=mesh,
        in_specs=(
            P(AXES, None),
            P(AXES, None),
            P(AXES),
            P("group", "member", None),
        ),
        out_specs=(P(AXES, None), P()),
        check_vma=False,
    )
```

```python
import functools

import jax
import jax.numpy as jnp
from jax import lax
from jax.experimental import pallas as pl
from jax.experimental.pallas import tpu as pltpu
from jax.sharding import PartitionSpec as P

EPS = 1e-06
AXES = ("group", "member")
F32 = jnp.float32
BF16 = jnp.bfloat16
META = 16
PIECES = 3


def units(raw):
    wide = raw.astype(F32)
    scale = lax.rsqrt(jnp.sum(wide * wide, axis=-1, keepdims=True) + EPS)
    return (wide * scale).astype(BF16), scale


def similarity(left, right):
    return lax.dot_general(left, right, (((1,), (1,)), ((), ())), preferred_element_type=F32)


def dot(left, right):
    return jnp.dot(left, right, preferred_element_type=F32)


def dot_transposed(left, right):
    return lax.dot_general(left, right, (((0,), (0,)), ((), ())), preferred_element_type=F32)


def column(row):
    wide = jnp.broadcast_to(row, (128, row.shape[1]))
    return jnp.transpose(wide)[:, :1]


def lanes(values):
    row = jnp.sum(values, axis=0, keepdims=True)
    return sum(row[:, k : k + 128] for k in range(0, row.shape[1], 128))


def weigh(mismatch, weight_column, weight_row):
    weight = weight_column * weight_row
    weighted = weight * mismatch
    return weighted.astype(BF16), lanes(weighted * mismatch), lanes(weight)


def tile(loss, weight):
    rows = lax.broadcasted_iota(jnp.int32, (8, 128), 0)
    zero = jnp.zeros((8, 128), F32)
    return jnp.where(rows == 0, loss, zero) + jnp.where(rows == 1, weight, zero)


class Packed:
    def __init__(self, first, second, rows, ds):
        self.first, self.second, self.rows, self.ds = first, second, rows, ds

    @property
    def s(self):
        return self.first[: self.rows, : self.ds]

    @property
    def t(self):
        return jnp.concatenate([self.first[: self.rows, self.ds :], self.second[...]], axis=1)

    def meta(self):
        return self.first[self.rows :, : self.ds].astype(F32)

    def counts(self, count=None):
        return self.meta()[0:1, : count or self.rows]

    def switch(self, if_even, if_odd):
        odd = lax.axis_index("member") % 2 == 1
        plan = self.meta()[1:2, :128]
        return jnp.where(odd, plan[:, if_odd : if_odd + 1], plan[:, if_even : if_even + 1])


def pack_kernel(counts_hbm, plan_hbm, s_hbm, t_hbm, both, first, second, student, numbers, scale, counts, plan, s, t, arrived):
    rows, ds = s.shape
    more = first.shape[1] - ds
    copies = [
        pltpu.make_async_copy(source, target, arrived.at[i])
        for i, (source, target) in enumerate(((s_hbm, s), (t_hbm, t), (counts_hbm, counts), (plan_hbm, plan)))
    ]
    for copy in copies:
        copy.start()
    copies[0].wait()
    unit, factor = units(s[...])
    scale[...] = jnp.broadcast_to(factor, scale.shape)
    student[...] = unit
    both[:, :ds] = unit
    first[:rows, :ds] = unit
    copies[1].wait()
    unit, _ = units(t[...])
    both[:, ds:] = unit
    first[:rows, ds:] = unit[:, :more]
    second[...] = unit[:, more:]

    def widen(values):
        return jnp.concatenate([values, jnp.zeros((1, first.shape[1] - values.shape[1]), F32)], axis=1)

    copies[2].wait()
    copies[3].wait()
    at = lax.broadcasted_iota(jnp.int32, (META, first.shape[1]), 0)
    meta = jnp.where(at == 0, widen(counts[...].astype(F32).reshape(1, rows)), 0.0)
    first[rows:] = jnp.where(at == 1, widen(plan[...].astype(F32)), meta).astype(BF16)
    numbers[...] = first[rows:, :ds]


def local_kernel(rows, ds, both, first, near_meta, near_student, near_teacher, mates, total, sums):
    own, near = Packed(first, None, rows, ds), Packed(near_meta, None, 0, ds)
    mates[:rows] = both[...]
    mates[rows:, :ds], _ = units(near_student[...])
    mates[rows:, ds:], _ = units(near_teacher[...])
    own_s, own_t, near_s, near_t = mates[:rows, :ds], mates[:rows, ds:], mates[rows:, :ds], mates[rows:, ds:]
    own_column = column(own.counts())
    mismatch = similarity(own_s, own_s) - similarity(own_t, own_t)
    coefficient, loss, weight = weigh(mismatch, own_column, own.counts())
    total[...] = dot(coefficient, own_s)
    mismatch = similarity(own_s, near_s) - similarity(own_t, near_t)
    coefficient, loss_2, weight_2 = weigh(mismatch, own_column, near.counts(rows) * own.switch(2, 0))
    total[...] += dot(coefficient, near_s)
    sums[...] = tile(loss + loss_2, weight + weight_2)


def cross_kernel(rows, ds, both, first, far_first, far_second, before, sums_before, total, give, sums):
    own, far = Packed(first, None, rows, ds), Packed(far_first, far_second, rows, ds)
    mismatch = similarity(both[:, :ds], far.s) - similarity(both[:, ds:], far.t)
    coefficient, loss, weight = weigh(mismatch, column(own.counts()), far.counts() * own.switch(4, 4))
    give[...] = dot_transposed(coefficient, both[:, :ds]).astype(BF16)
    total[...] = before[...] + dot(coefficient, far.s)
    sums[...] = sums_before[...] + tile(2.0 * loss, 2.0 * weight)


def ring_teacher_kernel(ds, mates, far, teacher_sim):
    unit, _ = units(far[...])
    teacher_sim[...] = similarity(unit, mates[:, ds:])


def ring_own_kernel(rows, ds, first, mates, teacher_sim, far_s, far_counts, coefficients, to_far, sums):
    own = Packed(first, None, rows, ds)
    mismatch = similarity(far_s[...], mates[:rows, :ds]) - teacher_sim[:, :rows]
    far_column = column(far_counts[...].astype(F32).reshape(1, rows))
    coefficients[...], loss, weight = weigh(mismatch, far_column, own.counts() * own.switch(3, 1))
    to_far[...] = dot(coefficients[...], mates[:rows, :ds]).astype(BF16)
    sums[...] = tile(2.0 * loss, 2.0 * weight)


def ring_near_kernel(
    rows, ds, near_meta, mates, teacher_sim, far_s, far_counts, coefficients, before, sums_before, sums_own,
    total, to_near, sums,
):
    near = Packed(near_meta, None, 0, ds)
    mismatch = similarity(far_s[...], mates[rows:, :ds]) - teacher_sim[:, rows:]
    far_column = column(far_counts[...].astype(F32).reshape(1, rows))
    near_coefficients, loss, weight = weigh(mismatch, far_column, near.counts(rows) * near.switch(2, 0))
    to_near[...] = dot_transposed(near_coefficients, far_s[...]).astype(BF16)
    total[...] = before[...] + dot_transposed(coefficients[...], far_s[...])
    result = sums_before[...] + sums_own[...] + tile(loss, weight)
    sums[...] = jnp.broadcast_to(jnp.concatenate([result[0:1], result[1:2]], axis=1), sums.shape)


def final_kernel(
    rows, ds, own, scale, total, from_near, from_far, from_cross, sums, grad, loss, result, result_loss, sent
):
    parts = jnp.sum(sums[...], axis=0, keepdims=True)
    loss_sum, weight_sum = (jnp.sum(parts[:, k : k + 128], axis=1, keepdims=True) for k in (0, 128))
    result_loss[...] = jnp.broadcast_to(ds * loss_sum / weight_sum, result_loss.shape)
    copies = [pltpu.make_async_copy(result_loss, loss, sent.at[PIECES])]
    copies[0].start()
    size = rows // PIECES
    for i in range(PIECES):
        piece = pl.ds(i * size, size)
        unit = own[piece].astype(F32)
        received = from_near[piece].astype(F32) + from_far[piece].astype(F32) + from_cross[piece].astype(F32)
        summed = total[piece] + received
        along = jnp.sum(summed * unit, axis=-1, keepdims=True)
        result[piece] = 4.0 * scale[piece, :1] * (summed - along * unit)
        copies.append(pltpu.make_async_copy(result.at[piece], grad.at[piece], sent.at[i]))
        copies[-1].start()
    for copy in copies:
        copy.wait()


def call(kernel, outs, vmem_mib, *operands, flops=0, **options):
    return pl.pallas_call(
        kernel,
        out_shape=outs,
        compiler_params=pltpu.CompilerParams(vmem_limit_bytes=vmem_mib << 20),
        cost_estimate=pl.CostEstimate(flops=flops, bytes_accessed=0, transcendentals=0),
        **options,
    )(*operands)


def per_device(student, teacher, counts, plan):
    groups, members = lax.axis_size("group"), lax.axis_size("member")
    rows, ds = student.shape
    dt = teacher.shape[1]

    def route(target):
        pairs = []
        for g in range(groups):
            for m in range(members):
                to_g, to_m = target(g, m)
                if to_g is not None:
                    pairs.append((g * members + m, to_g * members + to_m % members))
        return functools.partial(lax.ppermute, axis_name=AXES, perm=pairs)

    to_ring = route(lambda g, m: (g, m - 2 + 4 * (m % 2)))
    ring_back = route(lambda g, m: (g, m + 2 - 4 * (m % 2)))
    to_near = route(lambda g, m: (g, m ^ 1))
    to_cross = route(lambda g, m: (g ^ 1 if (g + m) % 2 == 0 else None, m))
    cross_back = route(lambda g, m: (g ^ 1 if (g + m) % 2 == 1 else None, m))

    f = jax.ShapeDtypeStruct
    acc, half, sums_shape = f((rows, ds), F32), f((rows, ds), BF16), f((8, 128), F32)

    def on_blocks(kernel):
        return functools.partial(kernel, rows, ds)

    ring_t, near_t, near_s = to_ring(teacher), to_near(teacher), to_near(student)
    width = (ds + dt) // 2
    both, first, second, own_s, own_meta, scale = call(
        pack_kernel,
        (
            f((rows, ds + dt), BF16), f((rows + META, width), BF16), f((rows, ds + dt - width), BF16),
            f((rows, ds), BF16), f((META, ds), BF16), f((rows, 128), F32),
        ),
        24,
        *(pltpu.with_memory_space_constraint(x, pltpu.HBM) for x in (counts, plan.reshape(1, -1), student, teacher)),
        in_specs=[pl.BlockSpec(memory_space=pltpu.HBM)] * 4,
        scratch_shapes=[
            pltpu.VMEM((rows,), jnp.int32),
            pltpu.VMEM((1, plan.size), jnp.int32),
            pltpu.VMEM((rows, ds), BF16),
            pltpu.VMEM((rows, dt), BF16),
            pltpu.SemaphoreType.DMA((4,)),
        ],
    )
    ring_s, ring_counts = to_ring(own_s), to_ring(counts)
    near_meta, cross = to_near(own_meta), (to_cross(first), to_cross(second))

    mates, total, sums = call(
        on_blocks(local_kernel), (f((2 * rows, ds + dt), BF16), acc, sums_shape), 24, both, first, near_meta, near_s, near_t
    )
    total, give_cross, sums = call(
        on_blocks(cross_kernel), (acc, half, sums_shape), 24, both, first, *cross, total, sums
    )
    from_cross = cross_back(give_cross)
    (teacher_sim,) = call(
        functools.partial(ring_teacher_kernel, ds), (f((rows, 2 * rows), F32),), 24, mates, ring_t
    )
    coefficients, give_ring, own_sums = call(
        on_blocks(ring_own_kernel), (f((rows, rows), BF16), half, sums_shape), 24,
        first, mates, teacher_sim, ring_s, ring_counts,
        flops=10**10,
    )
    from_ring = ring_back(give_ring)
    total, give_near, sums = call(
        on_blocks(ring_near_kernel), (acc, half, f((groups * members, 256), F32)), 24,
        near_meta, mates, teacher_sim, ring_s, ring_counts, coefficients, total, sums, own_sums,
    )
    sums, give_near, from_cross = lax.optimization_barrier((sums, give_near, from_cross))
    from_near = to_near(give_near)
    sums = lax.all_to_all(sums, AXES, 0, 0, tiled=True)
    grad, loss = call(
        on_blocks(final_kernel), (acc, f((1, 128), F32)), 24, own_s, scale, total, from_near, from_ring, from_cross, sums,
        out_specs=(pl.BlockSpec(memory_space=pltpu.HBM),) * 2,
        scratch_shapes=[
            pltpu.VMEM((rows, ds), F32), pltpu.VMEM((1, 128), F32), pltpu.SemaphoreType.DMA((PIECES + 1,)),
        ],
    )
    return grad, loss[0, 0]


def solution(mesh):
    return jax.shard_map(
        per_device,
        mesh=mesh,
        in_specs=(
            P(AXES, None),
            P(AXES, None),
            P(AXES),
            P("group", "member", None),
        ),
        out_specs=(P(AXES, None), P()),
        check_vma=False,
    )
```

```python
import functools

import jax
import jax.numpy as jnp
from jax import lax
from jax.experimental import pallas as pl
from jax.experimental.pallas import tpu as pltpu
from jax.sharding import PartitionSpec as P

EPS = 1e-06
AXES = ("group", "member")
F32 = jnp.float32
BF16 = jnp.bfloat16
META = 16
PIECES = 3


def units(raw):
    wide = raw.astype(F32)
    scale = lax.rsqrt(jnp.sum(wide * wide, axis=-1, keepdims=True) + EPS)
    return (wide * scale).astype(BF16), scale


def similarity(left, right):
    return lax.dot_general(left, right, (((1,), (1,)), ((), ())), preferred_element_type=F32)


def dot(left, right):
    return jnp.dot(left, right, preferred_element_type=F32)


def dot_transposed(left, right):
    return lax.dot_general(left, right, (((0,), (0,)), ((), ())), preferred_element_type=F32)


def column(row):
    wide = jnp.broadcast_to(row, (128, row.shape[1]))
    return jnp.transpose(wide)[:, :1]


def lanes(values):
    row = jnp.sum(values, axis=0, keepdims=True)
    return sum(row[:, k : k + 128] for k in range(0, row.shape[1], 128))


def weigh(mismatch, weight_column, weight_row):
    weight = weight_column * weight_row
    weighted = weight * mismatch
    weight_sum = lanes(weight_row * jnp.sum(weight_column, axis=0, keepdims=True))
    return weighted.astype(BF16), lanes(weighted * mismatch), weight_sum


def tile(loss, weight):
    rows = lax.broadcasted_iota(jnp.int32, (8, 128), 0)
    zero = jnp.zeros((8, 128), F32)
    return jnp.where(rows == 0, loss, zero) + jnp.where(rows == 1, weight, zero)


class Packed:
    def __init__(self, first, second, rows, ds):
        self.first, self.second, self.rows, self.ds = first, second, rows, ds

    @property
    def s(self):
        return self.first[: self.rows, : self.ds]

    @property
    def t(self):
        return jnp.concatenate([self.first[: self.rows, self.ds :], self.second[...]], axis=1)

    def meta(self):
        return self.first[self.rows :, : self.ds].astype(F32)

    def counts(self, count=None):
        return self.meta()[0:1, : count or self.rows]

    def switch(self, if_even, if_odd):
        odd = lax.axis_index("member") % 2 == 1
        plan = self.meta()[1:2, :128]
        return jnp.where(odd, plan[:, if_odd : if_odd + 1], plan[:, if_even : if_even + 1])


def pack_kernel(counts_hbm, plan_hbm, s_hbm, t_hbm, both, first, second, student, numbers, scale, counts, plan, s, t, arrived):
    rows, ds = s.shape
    more = first.shape[1] - ds
    copies = [
        pltpu.make_async_copy(source, target, arrived.at[i])
        for i, (source, target) in enumerate(((s_hbm, s), (t_hbm, t), (counts_hbm, counts), (plan_hbm, plan)))
    ]
    for copy in copies:
        copy.start()
    copies[0].wait()
    unit, factor = units(s[...])
    scale[...] = jnp.broadcast_to(factor, scale.shape)
    student[...] = unit
    both[:, :ds] = unit
    first[:rows, :ds] = unit
    copies[1].wait()
    unit, _ = units(t[...])
    both[:, ds:] = unit
    first[:rows, ds:] = unit[:, :more]
    second[...] = unit[:, more:]

    def widen(values):
        return jnp.concatenate([values, jnp.zeros((1, first.shape[1] - values.shape[1]), F32)], axis=1)

    copies[2].wait()
    copies[3].wait()
    at = lax.broadcasted_iota(jnp.int32, (META, first.shape[1]), 0)
    meta = jnp.where(at == 0, widen(counts[...].astype(F32).reshape(1, rows)), 0.0)
    first[rows:] = jnp.where(at == 1, widen(plan[...].astype(F32)), meta).astype(BF16)
    numbers[...] = first[rows:, :ds]


def local_kernel(rows, ds, both, first, near_meta, near_student, near_teacher, mates, total, sums):
    own, near = Packed(first, None, rows, ds), Packed(near_meta, None, 0, ds)
    mates[:rows] = both[...]
    mates[rows:, :ds], _ = units(near_student[...])
    mates[rows:, ds:], _ = units(near_teacher[...])
    own_s, own_t, near_s, near_t = mates[:rows, :ds], mates[:rows, ds:], mates[rows:, :ds], mates[rows:, ds:]
    own_column = column(own.counts())
    mismatch = similarity(own_s, own_s) - similarity(own_t, own_t)
    coefficient, loss, weight = weigh(mismatch, own_column, own.counts())
    total[...] = dot(coefficient, own_s)
    mismatch = similarity(own_s, near_s) - similarity(own_t, near_t)
    coefficient, loss_2, weight_2 = weigh(mismatch, own_column, near.counts(rows) * own.switch(2, 0))
    total[...] += dot(coefficient, near_s)
    sums[...] = tile(loss + loss_2, weight + weight_2)


def cross_kernel(rows, ds, both, first, far_first, far_second, before, sums_before, total, give, sums):
    own, far = Packed(first, None, rows, ds), Packed(far_first, far_second, rows, ds)
    mismatch = similarity(both[:, :ds], far.s) - similarity(both[:, ds:], far.t)
    coefficient, loss, weight = weigh(mismatch, column(own.counts()), far.counts() * own.switch(4, 4))
    give[...] = dot_transposed(coefficient, both[:, :ds]).astype(BF16)
    total[...] = before[...] + dot(coefficient, far.s)
    sums[...] = sums_before[...] + tile(2.0 * loss, 2.0 * weight)


def ring_teacher_kernel(ds, mates, far, teacher_sim):
    unit, _ = units(far[...])
    teacher_sim[...] = similarity(unit, mates[:, ds:])


def ring_own_kernel(rows, ds, first, mates, teacher_sim, far_s, far_counts, coefficients, to_far, sums):
    own = Packed(first, None, rows, ds)
    mismatch = similarity(far_s[...], mates[:rows, :ds]) - teacher_sim[:, :rows]
    far_column = column(far_counts[...].astype(F32).reshape(1, rows))
    coefficients[...], loss, weight = weigh(mismatch, far_column, own.counts() * own.switch(3, 1))
    to_far[...] = dot(coefficients[...], mates[:rows, :ds]).astype(BF16)
    sums[...] = tile(2.0 * loss, 2.0 * weight)


def ring_near_kernel(
    rows, ds, near_meta, mates, teacher_sim, far_s, far_counts, coefficients, before, sums_before, sums_own,
    total, to_near, sums,
):
    near = Packed(near_meta, None, 0, ds)
    mismatch = similarity(far_s[...], mates[rows:, :ds]) - teacher_sim[:, rows:]
    far_column = column(far_counts[...].astype(F32).reshape(1, rows))
    near_coefficients, loss, weight = weigh(mismatch, far_column, near.counts(rows) * near.switch(2, 0))
    to_near[...] = dot_transposed(near_coefficients, far_s[...]).astype(BF16)
    total[...] = before[...] + dot_transposed(coefficients[...], far_s[...])
    result = sums_before[...] + sums_own[...] + tile(loss, weight)
    sums[...] = jnp.broadcast_to(jnp.concatenate([result[0:1], result[1:2]], axis=1), sums.shape)


def final_kernel(
    rows, ds, own, scale, total, from_near, from_far, from_cross, sums, grad, loss, result, result_loss, sent
):
    parts = jnp.sum(sums[...], axis=0, keepdims=True)
    loss_sum, weight_sum = (jnp.sum(parts[:, k : k + 128], axis=1, keepdims=True) for k in (0, 128))
    result_loss[...] = jnp.broadcast_to(ds * loss_sum / weight_sum, result_loss.shape)
    copies = [pltpu.make_async_copy(result_loss, loss, sent.at[PIECES])]
    copies[0].start()
    size = rows // (PIECES * (PIECES + 1) // 2)
    for i in range(PIECES):
        piece = pl.ds(size * (i * (i + 1) // 2), size * (i + 1))
        unit = own[piece].astype(F32)
        received = from_near[piece].astype(F32) + from_far[piece].astype(F32) + from_cross[piece].astype(F32)
        summed = total[piece] + received
        along = jnp.sum(summed * unit, axis=-1, keepdims=True)
        result[piece] = 4.0 * scale[piece, :1] * (summed - along * unit)
        copies.append(pltpu.make_async_copy(result.at[piece], grad.at[piece], sent.at[i]))
        copies[-1].start()
    for copy in copies:
        copy.wait()


def call(kernel, outs, vmem_mib, *operands, flops=0, **options):
    return pl.pallas_call(
        kernel,
        out_shape=outs,
        compiler_params=pltpu.CompilerParams(vmem_limit_bytes=vmem_mib << 20),
        cost_estimate=pl.CostEstimate(flops=flops, bytes_accessed=0, transcendentals=0),
        **options,
    )(*operands)


def per_device(student, teacher, counts, plan):
    groups, members = lax.axis_size("group"), lax.axis_size("member")
    rows, ds = student.shape
    dt = teacher.shape[1]

    def route(target):
        pairs = []
        for g in range(groups):
            for m in range(members):
                to_g, to_m = target(g, m)
                if to_g is not None:
                    pairs.append((g * members + m, to_g * members + to_m % members))
        return functools.partial(lax.ppermute, axis_name=AXES, perm=pairs)

    to_ring = route(lambda g, m: (g, m - 2 + 4 * (m % 2)))
    ring_back = route(lambda g, m: (g, m + 2 - 4 * (m % 2)))
    to_near = route(lambda g, m: (g, m ^ 1))
    to_cross = route(lambda g, m: (g ^ 1 if (g + m) % 2 == 0 else None, m))
    cross_back = route(lambda g, m: (g ^ 1 if (g + m) % 2 == 1 else None, m))

    f = jax.ShapeDtypeStruct
    acc, half, sums_shape = f((rows, ds), F32), f((rows, ds), BF16), f((8, 128), F32)

    def on_blocks(kernel):
        return functools.partial(kernel, rows, ds)

    ring_t, near_t, near_s = to_ring(teacher), to_near(teacher), to_near(student)
    width = (ds + dt) // 2
    both, first, second, own_s, own_meta, scale = call(
        pack_kernel,
        (
            f((rows, ds + dt), BF16), f((rows + META, width), BF16), f((rows, ds + dt - width), BF16),
            f((rows, ds), BF16), f((META, ds), BF16), f((rows, 128), F32),
        ),
        24,
        *(pltpu.with_memory_space_constraint(x, pltpu.HBM) for x in (counts, plan.reshape(1, -1), student, teacher)),
        in_specs=[pl.BlockSpec(memory_space=pltpu.HBM)] * 4,
        scratch_shapes=[
            pltpu.VMEM((rows,), jnp.int32),
            pltpu.VMEM((1, plan.size), jnp.int32),
            pltpu.VMEM((rows, ds), BF16),
            pltpu.VMEM((rows, dt), BF16),
            pltpu.SemaphoreType.DMA((4,)),
        ],
    )
    ring_s, ring_counts = to_ring(own_s), to_ring(counts)
    near_meta, cross = to_near(own_meta), (to_cross(first), to_cross(second))

    mates, total, sums = call(
        on_blocks(local_kernel), (f((2 * rows, ds + dt), BF16), acc, sums_shape), 24, both, first, near_meta, near_s, near_t
    )
    total, give_cross, sums = call(
        on_blocks(cross_kernel), (acc, half, sums_shape), 24, both, first, *cross, total, sums
    )
    from_cross = cross_back(give_cross)
    (teacher_sim,) = call(
        functools.partial(ring_teacher_kernel, ds), (f((rows, 2 * rows), F32),), 24, mates, ring_t
    )
    coefficients, give_ring, own_sums = call(
        on_blocks(ring_own_kernel), (f((rows, rows), BF16), half, sums_shape), 24,
        first, mates, teacher_sim, ring_s, ring_counts,
        flops=10**10,
    )
    from_ring = ring_back(give_ring)
    total, give_near, sums = call(
        on_blocks(ring_near_kernel), (acc, half, f((groups * members, 256), F32)), 24,
        near_meta, mates, teacher_sim, ring_s, ring_counts, coefficients, total, sums, own_sums,
    )
    sums, give_near, from_cross = lax.optimization_barrier((sums, give_near, from_cross))
    from_near = to_near(give_near)
    sums = lax.all_to_all(sums, AXES, 0, 0, tiled=True)
    grad, loss = call(
        on_blocks(final_kernel), (acc, f((1, 128), F32)), 24, own_s, scale, total, from_near, from_ring, from_cross, sums,
        out_specs=(pl.BlockSpec(memory_space=pltpu.HBM),) * 2,
        scratch_shapes=[
            pltpu.VMEM((rows, ds), F32), pltpu.VMEM((1, 128), F32), pltpu.SemaphoreType.DMA((PIECES + 1,)),
        ],
    )
    return grad, loss[0, 0]


def solution(mesh):
    return jax.shard_map(
        per_device,
        mesh=mesh,
        in_specs=(
            P(AXES, None),
            P(AXES, None),
            P(AXES),
            P("group", "member", None),
        ),
        out_specs=(P(AXES, None), P()),
        check_vma=False,
    )
```

```python
import functools

import jax
import jax.numpy as jnp
from jax import lax
from jax.experimental import pallas as pl
from jax.experimental.pallas import tpu as pltpu
from jax.sharding import PartitionSpec as P

EPS = 1e-06
AXES = ("group", "member")
F32 = jnp.float32
BF16 = jnp.bfloat16
META = 16
PIECES = 3


def units(raw):
    wide = raw.astype(F32)
    scale = lax.rsqrt(jnp.sum(wide * wide, axis=-1, keepdims=True) + EPS)
    return (wide * scale).astype(BF16), scale


def similarity(left, right):
    return lax.dot_general(left, right, (((1,), (1,)), ((), ())), preferred_element_type=F32)


def dot(left, right):
    return jnp.dot(left, right, preferred_element_type=F32)


def dot_transposed(left, right):
    return lax.dot_general(left, right, (((0,), (0,)), ((), ())), preferred_element_type=F32)


def column(row):
    wide = jnp.broadcast_to(row, (128, row.shape[1]))
    return jnp.transpose(wide)[:, :1]


def lanes(values):
    row = jnp.sum(values, axis=0, keepdims=True)
    return sum(row[:, k : k + 128] for k in range(0, row.shape[1], 128))


def weigh(mismatch, weight_column, weight_row):
    weight = weight_column * weight_row
    weighted = weight * mismatch
    return weighted.astype(BF16), lanes(weighted * mismatch), lanes(weight)


def tile(loss, weight):
    rows = lax.broadcasted_iota(jnp.int32, (8, 128), 0)
    zero = jnp.zeros((8, 128), F32)
    return jnp.where(rows == 0, loss, zero) + jnp.where(rows == 1, weight, zero)


class Packed:
    def __init__(self, first, second, rows, ds):
        self.first, self.second, self.rows, self.ds = first, second, rows, ds

    @property
    def s(self):
        return self.first[: self.rows, : self.ds]

    @property
    def t(self):
        return jnp.concatenate([self.first[: self.rows, self.ds :], self.second[...]], axis=1)

    def meta(self):
        return self.first[self.rows :, : self.ds].astype(F32)

    def counts(self, count=None):
        return self.meta()[0:1, : count or self.rows]

    def switch(self, if_even, if_odd):
        odd = lax.axis_index("member") % 2 == 1
        plan = self.meta()[1:2, :128]
        return jnp.where(odd, plan[:, if_odd : if_odd + 1], plan[:, if_even : if_even + 1])


def pack_kernel(counts_hbm, plan_hbm, s_hbm, t_hbm, both, first, second, student, numbers, scale, counts, plan, s, t, arrived):
    rows, ds = s.shape
    more = first.shape[1] - ds
    copies = [
        pltpu.make_async_copy(source, target, arrived.at[i])
        for i, (source, target) in enumerate(((s_hbm, s), (t_hbm, t), (counts_hbm, counts), (plan_hbm, plan)))
    ]
    for copy in copies:
        copy.start()
    copies[0].wait()
    unit, factor = units(s[...])
    scale[...] = jnp.broadcast_to(factor, scale.shape)
    student[...] = unit
    both[:, :ds] = unit
    first[:rows, :ds] = unit
    copies[1].wait()
    unit, _ = units(t[...])
    both[:, ds:] = unit
    first[:rows, ds:] = unit[:, :more]
    second[...] = unit[:, more:]

    def widen(values):
        return jnp.concatenate([values, jnp.zeros((1, first.shape[1] - values.shape[1]), F32)], axis=1)

    copies[2].wait()
    copies[3].wait()
    at = lax.broadcasted_iota(jnp.int32, (META, first.shape[1]), 0)
    meta = jnp.where(at == 0, widen(counts[...].astype(F32).reshape(1, rows)), 0.0)
    first[rows:] = jnp.where(at == 1, widen(plan[...].astype(F32)), meta).astype(BF16)
    numbers[...] = first[rows:, :ds]


def local_kernel(rows, ds, both, first, near_meta, near_student, near_teacher, mates, total, sums):
    own, near = Packed(first, None, rows, ds), Packed(near_meta, None, 0, ds)
    mates[:rows] = both[...]
    mates[rows:, :ds], _ = units(near_student[...])
    mates[rows:, ds:], _ = units(near_teacher[...])
    own_s, own_t, near_s, near_t = mates[:rows, :ds], mates[:rows, ds:], mates[rows:, :ds], mates[rows:, ds:]
    own_column = column(own.counts())
    mismatch = similarity(own_s, own_s) - similarity(own_t, own_t)
    coefficient, loss, weight = weigh(mismatch, own_column, own.counts())
    total[...] = dot(coefficient, own_s)
    mismatch = similarity(own_s, near_s) - similarity(own_t, near_t)
    coefficient, loss_2, weight_2 = weigh(mismatch, own_column, near.counts(rows) * own.switch(2, 0))
    total[...] += dot(coefficient, near_s)
    sums[...] = tile(loss + loss_2, weight + weight_2)


def cross_kernel(rows, ds, both, first, far_first, far_second, before, sums_before, total, give, sums):
    own, far = Packed(first, None, rows, ds), Packed(far_first, far_second, rows, ds)
    mismatch = similarity(both[:, :ds], far.s) - similarity(both[:, ds:], far.t)
    coefficient, loss, weight = weigh(mismatch, column(own.counts()), far.counts() * own.switch(4, 4))
    give[...] = dot_transposed(coefficient, both[:, :ds]).astype(BF16)
    total[...] = before[...] + dot(coefficient, far.s)
    sums[...] = sums_before[...] + tile(2.0 * loss, 2.0 * weight)


def ring_teacher_kernel(ds, mates, far, teacher_sim):
    unit, _ = units(far[...])
    teacher_sim[...] = similarity(unit, mates[:, ds:])


def ring_own_kernel(rows, ds, first, mates, teacher_sim, far_s, far_counts, coefficients, to_far, sums):
    own = Packed(first, None, rows, ds)
    mismatch = similarity(far_s[...], mates[:rows, :ds]) - teacher_sim[:, :rows]
    far_column = column(far_counts[...].astype(F32).reshape(1, rows))
    coefficients[...], loss, weight = weigh(mismatch, far_column, own.counts() * own.switch(3, 1))
    to_far[...] = dot(coefficients[...], mates[:rows, :ds]).astype(BF16)
    sums[...] = tile(2.0 * loss, 2.0 * weight)


def ring_near_kernel(
    rows, ds, near_meta, mates, teacher_sim, far_s, far_counts, coefficients, before, sums_before, sums_own,
    total, to_near, sums,
):
    near = Packed(near_meta, None, 0, ds)
    mismatch = similarity(far_s[...], mates[rows:, :ds]) - teacher_sim[:, rows:]
    far_column = column(far_counts[...].astype(F32).reshape(1, rows))
    near_coefficients, loss, weight = weigh(mismatch, far_column, near.counts(rows) * near.switch(2, 0))
    to_near[...] = dot_transposed(near_coefficients, far_s[...]).astype(BF16)
    total[...] = before[...] + dot_transposed(coefficients[...], far_s[...])
    result = sums_before[...] + sums_own[...] + tile(loss, weight)
    sums[...] = jnp.broadcast_to(jnp.concatenate([result[0:1], result[1:2]], axis=1), sums.shape)


def final_kernel(
    rows, ds, own, scale, total, from_near, from_far, from_cross, sums, grad, loss, result, result_loss, sent
):
    parts = jnp.sum(sums[...], axis=0, keepdims=True)
    loss_sum, weight_sum = (jnp.sum(parts[:, k : k + 128], axis=1, keepdims=True) for k in (0, 128))
    result_loss[...] = jnp.broadcast_to(ds * loss_sum / weight_sum, result_loss.shape)
    copies = [pltpu.make_async_copy(result_loss, loss, sent.at[PIECES])]
    copies[0].start()
    size = rows // PIECES
    for i in range(PIECES):
        piece = pl.ds(i * size, size)
        unit = own[piece].astype(F32)
        received = from_near[piece].astype(F32) + from_far[piece].astype(F32) + from_cross[piece].astype(F32)
        summed = total[piece] + received
        along = jnp.sum(summed * unit, axis=-1, keepdims=True)
        result[piece] = 4.0 * scale[piece, :1] * (summed - along * unit)
        copies.append(pltpu.make_async_copy(result.at[piece], grad.at[piece], sent.at[i]))
        copies[-1].start()
    for copy in copies:
        copy.wait()


def call(kernel, outs, vmem_mib, *operands, flops=0, **options):
    return pl.pallas_call(
        kernel,
        out_shape=outs,
        compiler_params=pltpu.CompilerParams(vmem_limit_bytes=vmem_mib << 20),
        cost_estimate=pl.CostEstimate(flops=flops, bytes_accessed=0, transcendentals=0),
        **options,
    )(*operands)


def per_device(student, teacher, counts, plan):
    groups, members = lax.axis_size("group"), lax.axis_size("member")
    rows, ds = student.shape
    dt = teacher.shape[1]

    def route(target):
        pairs = []
        for g in range(groups):
            for m in range(members):
                to_g, to_m = target(g, m)
                if to_g is not None:
                    pairs.append((g * members + m, to_g * members + to_m % members))
        return functools.partial(lax.ppermute, axis_name=AXES, perm=pairs)

    to_ring = route(lambda g, m: (g, m - 2 + 4 * (m % 2)))
    ring_back = route(lambda g, m: (g, m + 2 - 4 * (m % 2)))
    to_near = route(lambda g, m: (g, m ^ 1))
    to_cross = route(lambda g, m: (g ^ 1 if (g + m) % 2 == 0 else None, m))
    cross_back = route(lambda g, m: (g ^ 1 if (g + m) % 2 == 1 else None, m))

    f = jax.ShapeDtypeStruct
    acc, half, sums_shape = f((rows, ds), F32), f((rows, ds), BF16), f((8, 128), F32)

    def on_blocks(kernel):
        return functools.partial(kernel, rows, ds)

    ring_t, near_t, near_s = to_ring(teacher), to_near(teacher), to_near(student)
    width = (ds + dt) // 2
    both, first, second, own_s, own_meta, scale = call(
        pack_kernel,
        (
            f((rows, ds + dt), BF16), f((rows + META, width), BF16), f((rows, ds + dt - width), BF16),
            f((rows, ds), BF16), f((META, ds), BF16), f((rows, 128), F32),
        ),
        24,
        *(pltpu.with_memory_space_constraint(x, pltpu.HBM) for x in (counts, plan.reshape(1, -1), student, teacher)),
        in_specs=[pl.BlockSpec(memory_space=pltpu.HBM)] * 4,
        scratch_shapes=[
            pltpu.VMEM((rows,), jnp.int32),
            pltpu.VMEM((1, plan.size), jnp.int32),
            pltpu.VMEM((rows, ds), BF16),
            pltpu.VMEM((rows, dt), BF16),
            pltpu.SemaphoreType.DMA((4,)),
        ],
    )
    ring_s, ring_counts = to_ring(own_s), to_ring(counts)
    near_meta, cross = to_near(own_meta), (to_cross(first), to_cross(second))

    mates, total, sums = call(
        on_blocks(local_kernel), (f((2 * rows, ds + dt), BF16), acc, sums_shape), 24, both, first, near_meta, near_s, near_t
    )
    total, give_cross, sums = call(
        on_blocks(cross_kernel), (acc, half, sums_shape), 24, both, first, *cross, total, sums
    )
    from_cross = cross_back(give_cross)
    (teacher_sim,) = call(
        functools.partial(ring_teacher_kernel, ds), (f((rows, 2 * rows), F32),), 24, mates, ring_t, flops=10**10
    )
    coefficients, give_ring, own_sums = call(
        on_blocks(ring_own_kernel), (f((rows, rows), BF16), half, sums_shape), 24,
        first, mates, teacher_sim, ring_s, ring_counts,
    )
    from_ring = ring_back(give_ring)
    total, give_near, sums = call(
        on_blocks(ring_near_kernel), (acc, half, f((groups * members, 256), F32)), 24,
        near_meta, mates, teacher_sim, ring_s, ring_counts, coefficients, total, sums, own_sums,
    )
    sums, give_near, from_cross = lax.optimization_barrier((sums, give_near, from_cross))
    from_near = to_near(give_near)
    sums = lax.all_to_all(sums, AXES, 0, 0, tiled=True)
    grad, loss = call(
        on_blocks(final_kernel), (acc, f((1, 128), F32)), 24, own_s, scale, total, from_near, from_ring, from_cross, sums,
        out_specs=(pl.BlockSpec(memory_space=pltpu.HBM),) * 2,
        scratch_shapes=[
            pltpu.VMEM((rows, ds), F32), pltpu.VMEM((1, 128), F32), pltpu.SemaphoreType.DMA((PIECES + 1,)),
        ],
    )
    return grad, loss[0, 0]


def solution(mesh):
    return jax.shard_map(
        per_device,
        mesh=mesh,
        in_specs=(
            P(AXES, None),
            P(AXES, None),
            P(AXES),
            P("group", "member", None),
        ),
        out_specs=(P(AXES, None), P()),
        check_vma=False,
    )
```
